32 devices in a mesh: batch: 4 (over y, core), lat: 8 (over z, x).
Axes of the slice: x: 2, y: 2, z: 4, core: 2. Of those that a mesh axis runs over, the one named last changes fastest.
Arguments:
- adjoint_in: float32 [80, 60, 16, 128], P('batch', None, 'lat'), may hold values from -6 to 6
- east_courant: bfloat16 [4, 60, 16, 128], P('batch', None, 'lat'), may hold values from -0.8984375 to 0.8984375
- north_courant: bfloat16 [4, 60, 16, 128], P('batch', None, 'lat'), may hold values from -0.8984375 to 0.8984375
- convection: bfloat16 [4, 60, 60, 16, 128], P('batch', None, None, 'lat'), may hold values from 0 to 1, as said below
- hour_owner: int32 [4, 16], P(None, 'lat'), may hold values from 0 to 3, as said below
- obs_lat: int32 [80], P('batch'), may hold values from 0 to 15
- obs_lon: int32 [80], P('batch'), may hold values from 0 to 127
- obs_level: int32 [80], P('batch'), may hold values from 0 to 59
- obs_hour: int32 [80], P('batch'), may hold values from 0 to 1
- misfit: float32 [80], P('batch'), may hold values from -8 to 8
Outputs:
- adjoint_out: float32 [80, 60, 16, 128], P('batch', None, 'lat')
- emission_grad: float32 [16, 128], P('lat')
The draws below stay inside these ranges and needn't reach their ends.
Inputs may be any that keep to these rules, and one draw needn't show every extreme that they name: Each column hour_owner[:, y] names every slot once; the 2 rows of one latitude device share their column. `convection`: nonnegative entries.
All inputs are finite; a program needn't handle non-finite values.
Results may differ from the reference program's by a relative error of at most 0.0039.
Values may be sent and summed in bfloat16 or wider, within the bound.
A program may use at most 128 MiB of HBM per device.

```python
import math
import jax
import jax.numpy as jnp
from jax import lax

LEV = 60
NLON = 128
CL = 2
HOURS = 2
TR = 80
NLAT = 16
N_BATCH = 4


def draw_convection(key, part):
    key = jax.random.fold_in(key, 11)
    shape = (N_BATCH, LEV, LEV, NLAT, NLON)
    diagonal = jax.lax.broadcasted_iota(jnp.int32, shape, 1) == jax.lax.broadcasted_iota(jnp.int32, shape, 2)
    main = jnp.full(shape, 0.6, jnp.float32)
    off = jax.random.uniform(key, shape, jnp.float32, 0.0, 0.8 / LEV)
    return jnp.where(diagonal, main, off).astype(jnp.bfloat16)


def draw_hour_owner(key, part):
    key = jax.random.fold_in(key, 23)
    slabs = NLAT // CL
    scores = jax.random.randint(key, (N_BATCH, slabs), 0, 1 << 20) * N_BATCH
    scores = scores + jax.lax.broadcasted_iota(jnp.int32, (N_BATCH, slabs), 0)
    order = jnp.argsort(scores, axis=0, stable=True).astype(jnp.int32)
    return jnp.repeat(order, CL, axis=1)


def touch_ends(values, key, low, largest):
    longest = values.shape.index(max(values.shape))
    spots = []
    for shift in (0, 1):
        where = [jax.random.randint(jax.random.fold_in(key, axis), (), 0, length) for axis, length in enumerate(values.shape)]
        where[longest] = (where[longest] + shift) % values.shape[longest]
        spots.append(tuple(where))
    return values.at[spots[0]].set(low).at[spots[1]].set(largest)


def level_of(rng, shape, shards, low, largest):
    def one(dim, blocks):
        draws = jax.random.uniform(jax.random.fold_in(jax.random.fold_in(rng, 6), dim), (blocks,), jnp.float32, low / len(shards), largest / len(shards))
        return jnp.repeat(jnp.exp(draws), shape[dim] // blocks).reshape((-1,) + (1,) * (len(shape) - dim - 1))

    level = one(*shards[0])
    for cut in shards[1:]:
        level = level * one(*cut)
    return level


def bell_draw(rng, extent, spread, most, shards=(), kind=jnp.bfloat16):
    entries = spread * jax.random.normal(rng, extent, jnp.float32)
    if shards:
        entries = entries * level_of(rng, extent, shards, -0.22, 0.18)
    return jnp.clip(entries, -most, most).astype(kind)


def setup_inputs(seed: int = 0) -> dict:
    arg_keys = jax.random.split(jax.random.key(seed), 11)
    adjoint_in = bell_draw(arg_keys[0], (TR, LEV, NLAT, NLON), 1.0, 6.0, ((0, 4), (2, 8)), jnp.float32)
    east_courant = jnp.clip(jax.random.uniform(arg_keys[1], (N_BATCH, LEV, NLAT, NLON), jnp.float32, -0.8984375, 0.8984375) * level_of(arg_keys[1], (N_BATCH, LEV, NLAT, NLON), ((0, 4), (2, 8)), -0.4, 0.0), -0.8984375, 0.8984375).astype(jnp.bfloat16)
    north_courant = jnp.clip(jax.random.uniform(arg_keys[2], (N_BATCH, LEV, NLAT, NLON), jnp.float32, -0.8984375, 0.8984375) * level_of(arg_keys[2], (N_BATCH, LEV, NLAT, NLON), ((0, 4), (2, 8)), -0.4, 0.0), -0.8984375, 0.8984375).astype(jnp.bfloat16)
    convection = draw_convection(jax.random.fold_in(arg_keys[10], 71), 0)
    hour_owner = draw_hour_owner(jax.random.fold_in(arg_keys[10], 71), 0)
    obs_lat = touch_ends(jax.random.randint(arg_keys[5], (TR,), 0, NLAT), jax.random.fold_in(arg_keys[5], 1), 0, NLAT - 1).astype(jnp.int32)
    obs_lon = touch_ends(jax.random.randint(arg_keys[6], (TR,), 0, NLON), jax.random.fold_in(arg_keys[6], 1), 0, NLON - 1).astype(jnp.int32)
    obs_level = touch_ends(jax.random.randint(arg_keys[7], (TR,), 0, LEV), jax.random.fold_in(arg_keys[7], 1), 0, LEV - 1).astype(jnp.int32)
    obs_hour = touch_ends(jax.random.randint(arg_keys[8], (TR,), 0, HOURS), jax.random.fold_in(arg_keys[8], 1), 0, HOURS - 1).astype(jnp.int32)
    misfit = bell_draw(arg_keys[9], (TR,), 2.0, 8.0, ((0, 4),), jnp.float32)
    return {"adjoint_in": adjoint_in, "east_courant": east_courant, "north_courant": north_courant, "convection": convection, "hour_owner": hour_owner, "obs_lat": obs_lat, "obs_lon": obs_lon, "obs_level": obs_level, "obs_hour": obs_hour, "misfit": misfit}


def coefficients(courant):
    pos_part = jnp.maximum(courant, 0.0)
    neg_part = jnp.minimum(courant, 0.0)
    return (pos_part, neg_part, pos_part * (1.0 - pos_part) * 0.5, neg_part * (1.0 + neg_part) * 0.5)

def cut_range(array, begin, end, axis):
    return lax.slice_in_dim(array, begin, end, axis=axis)

def adjoint_core(padded, courant, axis, count):
    jump = cut_range(padded, 1, count + 4, axis) - cut_range(padded, 0, count + 3, axis)
    pos_part, neg_part, pos_term, neg_term = coefficients(cut_range(courant, 0, count + 3, axis))
    slope_terms = cut_range(pos_term, 1, count + 3, axis) * cut_range(jump, 1, count + 3, axis) - cut_range(neg_term, 0, count + 2, axis) * cut_range(jump, 0, count + 2, axis)
    result = cut_range(padded, 2, count + 2, axis)
    result = result + cut_range(pos_part, 2, count + 2, axis) * cut_range(jump, 2, count + 2, axis)
    result = result + cut_range(neg_part, 1, count + 1, axis) * cut_range(jump, 1, count + 1, axis)
    return result + 0.5 * (cut_range(slope_terms, 0, count, axis) - cut_range(slope_terms, 2, count + 2, axis))

def zero_pad(array, axis):
    widths = [(0, 0)] * array.ndim
    widths[axis] = (2, 2)
    return jnp.pad(array, widths)

def pick_rows(table, slot_rows):
    shape = (1,) + table.shape[1:]
    index = jnp.broadcast_to(slot_rows.astype(jnp.int32).reshape((1,) * (table.ndim - 2) + (NLAT, 1)), shape)
    return jnp.take_along_axis(table, index, axis=0)[0]

def reference(adjoint_in, east_courant, north_courant, convection, hour_owner, obs_lat, obs_lon, obs_level, obs_hour, misfit):
    lev_ids = jnp.arange(LEV, dtype=jnp.int32)[:, None, None]
    row_ids = jnp.arange(NLAT, dtype=jnp.int32)[None, :, None]
    lon_ids = jnp.arange(NLON, dtype=jnp.int32)[None, None, :]
    adjoint = adjoint_in
    grad = jnp.zeros((NLAT, NLON), jnp.float32)
    for hour in reversed(range(HOURS)):
        slot_rows = hour_owner[hour]
        east = pick_rows(east_courant, slot_rows).astype(jnp.float32)
        north = pick_rows(north_courant, slot_rows).astype(jnp.float32)
        north = jnp.where(row_ids == NLAT - 1, 0.0, north)
        mixing = pick_rows(convection, slot_rows).astype(jnp.float32)
        east_pad = zero_pad(east, 2)
        north_pad = zero_pad(north, 1)

        def one_tracer(inputs):
            field, lat_at, lon_at, level_at, hour_at, weight = inputs
            hit = (lev_ids == level_at) & (row_ids == lat_at) & (lon_ids == lon_at) & (hour_at == hour)
            field = field + jnp.where(hit, weight, 0.0)
            field = adjoint_core(zero_pad(field, 2), east_pad, 2, NLON)
            field = adjoint_core(zero_pad(field, 1), north_pad, 1, NLAT)
            rounded = lax.optimization_barrier(field.astype(jnp.bfloat16)).astype(jnp.float32)
            return jnp.einsum('mkyx,myx->kyx', mixing, rounded, precision=lax.Precision.HIGHEST)
        adjoint = lax.map(one_tracer, (adjoint, obs_lat, obs_lon, obs_level, obs_hour, misfit))
        grad = grad + lax.optimization_barrier(jnp.sum(adjoint[:, 0], axis=0))
    return (adjoint, grad * (1.0 / math.sqrt(TR)))
```

```python
import functools
import math

import jax
import jax.numpy as jnp
from jax import lax
from jax.experimental import pallas as pl
from jax.experimental.pallas import tpu as pltpu
from jax.sharding import PartitionSpec as P

HOURS = 2
F32 = jnp.float32
BF16 = jnp.bfloat16
VMEM_LIMIT = 56 * 1024 * 1024


def divisor(value, most):
    return max(d for d in range(1, most + 1) if value % d == 0)


def remote(src, dst, send, recv, where):
    return pltpu.make_async_remote_copy(
        src_ref=src,
        dst_ref=dst,
        send_sem=send,
        recv_sem=recv,
        device_id=where,
        device_id_type=pl.DeviceIdType.MESH,
    )


def faces(courant):
    pos = jnp.maximum(courant, 0.0)
    neg = jnp.minimum(courant, 0.0)
    return pos, neg, pos * (1.0 - pos) * 0.25, neg * (1.0 + neg) * 0.25


def stencil(here, before, before2, after):
    pos, neg, _, neg_slope = faces(here)
    alpha = pos + neg_slope
    _, neg_before, pos_slope_before, _ = faces(before)
    beta = neg_before + pos_slope_before
    q = faces(before2)[3]
    p = faces(after)[2]
    return q, -beta - q, 1.0 - alpha + beta, alpha + p, -p


def kernel(
    n,
    n_lat,
    tracers,
    levels,
    rows,
    block,
    chunk,
    scale,
    adj,
    met,
    conv,
    owner,
    obs_lat,
    obs_lon,
    obs_level,
    obs_hour,
    misfit,
    out,
    grad_out,
    table,
    ring_c,
    north_sel,
    coef_e,
    coef_n,
    send_h,
    halo,
    east_f,
    rounded,
    exch,
    stage_s,
    stage_r,
    mix_b,
    mix_f,
    grad_all,
    s_met,
    r_met,
    s_ring,
    r_ring,
    s_halo,
    r_halo,
    s_exch,
    r_exch,
    s_stage,
    r_stage,
    s_fwd,
    r_fwd,
    s_grad,
    r_grad,
):
    me = lax.axis_index("batch")
    lat = lax.axis_index("lat")
    core = lax.rem(me, 2)
    mate = me + 1 - 2 * core
    bits = []
    bit = 2
    while bit < n:
        bits.append(bit)
        bit *= 2
    n_stage = len(bits)
    half = levels // 2
    n_chunk = half // chunk
    height = levels * rows
    width = adj.shape[-1]
    tiles = height // 8
    n_block = tracers // block
    first = core * half
    other = (1 - core) * half
    up = {"lat": lat + 1}
    down = {"lat": lat - 1}
    has_up = lat < n_lat - 1
    has_down = lat > 0

    barrier = pltpu.get_barrier_semaphore()
    for k in range(1, n):
        pl.semaphore_signal(
            barrier, inc=1, device_id={"batch": lax.rem(me + k, n)}, device_id_type=pl.DeviceIdType.MESH
        )

    @pl.when(has_up)
    def _():
        pl.semaphore_signal(barrier, inc=1, device_id=up, device_id_type=pl.DeviceIdType.MESH)

    @pl.when(has_down)
    def _():
        pl.semaphore_signal(barrier, inc=1, device_id=down, device_id_type=pl.DeviceIdType.MESH)

    pl.semaphore_wait(barrier, n - 1 + jnp.where(has_up, 1, 0) + jnp.where(has_down, 1, 0))

    def met_copy(k):
        return remote(
            met, table.at[me], s_met.at[k], r_met.at[k], {"batch": lax.rem(me + k, n)}
        )

    for k in range(1, n):
        met_copy(k).start()

    def exch_copy(j):
        return remote(
            conv.at[pl.ds(other + j * chunk, chunk)],
            exch.at[pl.ds(j * chunk, chunk)],
            s_exch.at[j],
            r_exch.at[j],
            {"batch": mate},
        )

    for j in range(n_chunk):
        exch_copy(j).start()

    table[me] = met[...]

    def zero_halo(side):
        ring_c[side] = jnp.zeros(ring_c.shape[1:], BF16)

        def body(t, carry):
            for hour in range(HOURS):
                halo[hour, side, t] = jnp.zeros(halo.shape[3:], BF16)
            return carry

        lax.fori_loop(0, tracers, body, 0)

    @pl.when(jnp.logical_not(has_down))
    def _():
        zero_halo(0)

    @pl.when(jnp.logical_not(has_up))
    def _():
        zero_halo(1)

    for k in range(1, n):
        met_copy(k).wait_recv()

    line = lax.broadcasted_iota(jnp.int32, (height, width), 0)
    lane = lax.broadcasted_iota(jnp.int32, (height, width), 1)
    row_of = lax.rem(line, rows) + lat * rows
    even8 = lax.rem(lax.broadcasted_iota(jnp.int32, (tiles, 8, width), 1), 2) == 0

    def swap(value):
        tall = value.reshape(tiles, 8, width)
        mixed = jnp.where(even8, pltpu.roll(tall, 7, 1), pltpu.roll(tall, 1, 1))
        return mixed.reshape(height, width)

    even = lax.rem(line, 2) == 0

    for hour in range(HOURS):
        north = table[owner[hour], 1].astype(F32)
        north = jnp.where(row_of == n_lat * rows - 1, 0.0, north)
        north_sel[hour] = north.astype(BF16)

    def ring_copies(side):
        return remote(
            north_sel, ring_c.at[side], s_ring.at[side], r_ring.at[side], up if side == 0 else down
        )

    @pl.when(has_up)
    def _():
        ring_copies(0).start()

    @pl.when(has_down)
    def _():
        ring_copies(1).start()

    for hour in range(HOURS):
        ce = table[owner[hour], 0].astype(F32)
        before = jnp.where(lane >= 1, pltpu.roll(ce, 1, 1), 0.0)
        before2 = jnp.where(lane >= 2, pltpu.roll(ce, 2, 1), 0.0)
        after = jnp.where(lane < width - 1, pltpu.roll(ce, width - 1, 1), 0.0)
        weights = stencil(ce, before, before2, after)
        inside = (lane >= 2, lane >= 1, None, lane < width - 1, lane < width - 2)
        for i, (weight, keep) in enumerate(zip(weights, inside)):
            coef_e[hour, i] = weight if keep is None else jnp.where(keep, weight, 0.0)

    def halo_copy(hour, side, tb):
        at = pl.ds(tb * block, block)
        return remote(
            send_h.at[hour, at],
            halo.at[hour, side, at],
            s_halo.at[hour, side, tb],
            r_halo.at[hour, side, tb],
            up if side == 0 else down,
        )

    def east_sweep(hour, tb, source):
        def body(i, carry):
            t = tb * block + i
            row_at = obs_lat[t] - lat * rows
            local = (row_at >= 0) & (row_at < rows) & (obs_hour[t] == hour)
            add = jnp.where(local, misfit[t], 0.0)
            hit = (line == obs_level[t] * rows + row_at) & (lane == obs_lon[t])
            field = source[t] + jnp.where(hit, add, 0.0)
            total = coef_e[hour, 2] * field
            total += coef_e[hour, 0] * pltpu.roll(field, 2, 1)
            total += coef_e[hour, 1] * pltpu.roll(field, 1, 1)
            total += coef_e[hour, 3] * pltpu.roll(field, width - 1, 1)
            total += coef_e[hour, 4] * pltpu.roll(field, width - 2, 1)
            east_f[t] = total
            send_h[hour, t] = total.astype(BF16)
            return carry

        lax.fori_loop(0, block, body, 0)

        @pl.when(has_up)
        def _():
            halo_copy(hour, 0, tb).start()

        @pl.when(has_down)
        def _():
            halo_copy(hour, 1, tb).start()

    def north_sweep(hour, tb):
        @pl.when(has_down)
        def _():
            halo_copy(hour, 0, tb).wait_recv()

        @pl.when(has_up)
        def _():
            halo_copy(hour, 1, tb).wait_recv()

        def body(i, carry):
            t = tb * block + i
            field = east_f[t]
            below = halo[hour, 0, t].astype(F32)
            above = halo[hour, 1, t].astype(F32)
            total = coef_n[hour, 0] * below + coef_n[hour, 1] * field
            total += coef_n[hour, 2] * above
            total += coef_n[hour, 3] * swap(field)
            total += coef_n[hour, 4] * swap(jnp.where(even, above, below))
            rounded[t] = total.astype(BF16).astype(F32)
            return carry

        lax.fori_loop(0, block, body, 0)

    even1 = lax.rem(lax.broadcasted_iota(jnp.int32, (1, 8, width), 1), 2) == 0
    part = divisor(tiles, 5)

    def mix(hour, tb):
        t_at = pl.ds(tb * block, block)

        def strip(s, carry):
            at = pl.ds(pl.multiple_of(s * part * 8, 8), part * 8)

            def step(g, acc):
                for q in range(4):
                    m = g * 4 + q
                    base = pl.multiple_of(g * 8, 8)
                    low = rounded[t_at, pl.ds(base + 2 * q, 1), :]
                    high = rounded[t_at, pl.ds(base + 2 * q + 1, 1), :]
                    pair = jnp.where(even1, low, high)
                    matrix = mix_f[hour, m, at, :].reshape(1, part, 8, width)
                    acc = acc + matrix * pair[:, None]
                return acc

            acc = lax.fori_loop(0, levels // 4, step, jnp.zeros((block, part, 8, width), F32))
            out[t_at, at, :] = acc.reshape(block, part * 8, width)
            return carry

        lax.fori_loop(0, tiles // part, strip, 0)

    def stage_copy(s, hour, j):
        at = pl.ds(j * chunk, chunk)
        bit = bits[s]
        return remote(
            stage_s.at[s, hour, at],
            stage_r.at[s, hour, at],
            s_stage.at[s, hour, j],
            r_stage.at[s, hour, j],
            {"batch": me + bit * (1 - 2 * lax.rem(me // bit, 2))},
        )

    def fwd_copy(hour, j, start):
        at = pl.ds(start + j * chunk, chunk)
        return remote(
            mix_b.at[hour, at],
            mix_b.at[hour, at],
            s_fwd.at[hour, j],
            r_fwd.at[hour, j],
            {"batch": mate},
        )

    def pick(flag, a, b):
        return lax.select(flag, a, b)

    def fill_stage(hour, j):
        at = pl.ds(j * chunk, chunk)
        mine = lax.rem(owner[hour], 2) == core
        stage_s[0, hour, at] = pick(mine, conv[pl.ds(first + j * chunk, chunk)], exch[at])

    def receive(hour, s):
        bit = bits[s]
        mine = lax.rem(owner[hour] // bit, 2) == lax.rem(me // bit, 2)

        def body(j, carry):
            at = pl.ds(j * chunk, chunk)
            stage_copy(s, hour, j).wait_recv()
            value = pick(mine, stage_s[s, hour, at], stage_r[s, hour, at])
            if s + 1 < n_stage:
                stage_s[s + 1, hour, at] = value
                stage_copy(s + 1, hour, j).start()
            else:
                mix_b[hour, pl.ds(first + j * chunk, chunk)] = value
                fwd_copy(hour, j, first).start()
                mix_f[hour, pl.ds(first + j * chunk, chunk)] = value.astype(F32)
            if s == 0 and hour > 0:
                stage_copy(0, hour - 1, j).start()
            return carry

        lax.fori_loop(0, n_chunk, body, 0)

    def widen(hour):
        def body(j, carry):
            at = pl.ds(other + j * chunk, chunk)
            fwd_copy(hour, j, other).wait_recv()
            mix_f[hour, at] = mix_b[hour, at].astype(F32)
            return carry

        lax.fori_loop(0, n_chunk, body, 0)

    last = HOURS - 1
    for tb in range(n_block):
        east_sweep(last, tb, adj)

    def start_stage(j, carry):
        exch_copy(j).wait_recv()
        fill_stage(last, j)
        stage_copy(0, last, j).start()
        for hour in range(last):
            fill_stage(hour, j)
        return carry

    lax.fori_loop(0, n_chunk, start_stage, 0)

    @pl.when(has_down)
    def _():
        ring_copies(0).wait_recv()

    @pl.when(has_up)
    def _():
        ring_copies(1).wait_recv()

    for hour in range(HOURS):
        here = north_sel[hour].astype(F32)
        below = ring_c[0, hour].astype(F32)
        above = ring_c[1, hour].astype(F32)
        turned = swap(here)
        crossed = swap(jnp.where(even, above, below))
        before = jnp.where(even, crossed, turned)
        after = jnp.where(even, turned, crossed)
        w_m2, w_m1, w_0, w_p1, w_p2 = stencil(here, before, below, after)
        coef_n[hour, 0] = w_m2
        coef_n[hour, 1] = w_0
        coef_n[hour, 2] = w_p2
        coef_n[hour, 3] = jnp.where(even, w_p1, w_m1)
        coef_n[hour, 4] = jnp.where(even, w_m1, w_p1)

    early = n_block // 2
    for tb in range(early):
        north_sweep(last, tb)

    surface = jnp.zeros((8, width), F32)
    for hour in reversed(range(HOURS)):
        for s in range(n_stage):
            receive(hour, s)
        widen(hour)
        for tb in range(n_block):
            if hour < last or tb >= early:
                north_sweep(hour, tb)
            mix(hour, tb)
            for i in range(block):
                surface = surface + out[tb * block + i, 0:8, :]
            if hour > 0:
                east_sweep(hour - 1, tb, out)

    grad_all[me] = surface

    def grad_copy(k):
        return remote(
            grad_all.at[me],
            grad_all.at[me],
            s_grad.at[k],
            r_grad.at[k],
            {"batch": lax.rem(me + k, n)},
        )

    for k in range(1, n):
        grad_copy(k).start()

    for k in range(1, n):
        met_copy(k).wait_send()

    @pl.when(has_up)
    def _():
        ring_copies(0).wait_send()
        for hour in range(HOURS):
            for tb in range(n_block):
                halo_copy(hour, 0, tb).wait_send()

    @pl.when(has_down)
    def _():
        ring_copies(1).wait_send()
        for hour in range(HOURS):
            for tb in range(n_block):
                halo_copy(hour, 1, tb).wait_send()

    def drain(j, carry):
        exch_copy(j).wait_send()
        for hour in range(HOURS):
            for s in range(n_stage):
                stage_copy(s, hour, j).wait_send()
            fwd_copy(hour, j, first).wait_send()
        return carry

    lax.fori_loop(0, n_chunk, drain, 0)
    for k in range(1, n):
        grad_copy(k).wait_recv()
    for k in range(1, n):
        grad_copy(k).wait_send()
    total = grad_all[0]
    for k in range(1, n):
        total = total + grad_all[k]
    grad_out[...] = total[0:rows] * scale


def on_device(
    adjoint_in,
    east_courant,
    north_courant,
    convection,
    hour_owner,
    obs_lat,
    obs_lon,
    obs_level,
    obs_hour,
    misfit,
):
    tracers, levels, rows, width = adjoint_in.shape
    n = lax.axis_size("batch")
    n_lat = lax.axis_size("lat")
    height = levels * rows
    block = divisor(tracers, 5)
    half = levels // 2
    chunk = divisor(half, 5)
    n_chunk = half // chunk
    n_block = tracers // block
    n_stage = n.bit_length() - 2
    scale = 1.0 / math.sqrt(tracers * n)
    met = jnp.concatenate([east_courant, north_courant], axis=0).reshape(2, height, width)
    vmem = pl.BlockSpec(memory_space=pltpu.VMEM)
    smem = pl.BlockSpec(memory_space=pltpu.SMEM)
    dma = pltpu.SemaphoreType.DMA
    body = functools.partial(
        kernel, n, n_lat, tracers, levels, rows, block, chunk, scale
    )
    out, grad = pl.pallas_call(
        body,
        out_shape=(
            jax.ShapeDtypeStruct((tracers, height, width), F32),
            jax.ShapeDtypeStruct((rows, width), F32),
        ),
        in_specs=[vmem] * 3 + [smem] * 6,
        out_specs=(vmem, vmem),
        scratch_shapes=[
            pltpu.VMEM((n, 2, height, width), BF16),
            pltpu.VMEM((2, HOURS, height, width), BF16),
            pltpu.VMEM((HOURS, height, width), BF16),
            pltpu.VMEM((HOURS, 5, height, width), F32),
            pltpu.VMEM((HOURS, 5, height, width), F32),
            pltpu.VMEM((HOURS, tracers, height, width), BF16),
            pltpu.VMEM((HOURS, 2, tracers, height, width), BF16),
            pltpu.VMEM((tracers, height, width), F32),
            pltpu.VMEM((tracers, height, width), F32),
            pltpu.VMEM((half, height, width), BF16),
            pltpu.VMEM((n_stage, HOURS, half, height, width), BF16),
            pltpu.VMEM((n_stage, HOURS, half, height, width), BF16),
            pltpu.VMEM((HOURS, levels, height, width), BF16),
            pltpu.VMEM((HOURS, levels, height, width), F32),
            pltpu.VMEM((n, 8, width), F32),
            dma((n,)),
            dma((n,)),
            dma((2,)),
            dma((2,)),
            dma((HOURS, 2, n_block)),
            dma((HOURS, 2, n_block)),
            dma((n_chunk,)),
            dma((n_chunk,)),
            dma((n_stage, HOURS, n_chunk)),
            dma((n_stage, HOURS, n_chunk)),
            dma((HOURS, n_chunk)),
            dma((HOURS, n_chunk)),
            dma((n,)),
            dma((n,)),
        ],
        compiler_params=pltpu.CompilerParams(
            collective_id=0, has_side_effects=True, vmem_limit_bytes=VMEM_LIMIT
        ),
    )(
        adjoint_in.reshape(tracers, height, width),
        met,
        convection.reshape(levels, height, width),
        hour_owner[:HOURS, 0],
        obs_lat,
        obs_lon,
        obs_level,
        obs_hour,
        misfit,
    )
    return (out.reshape(tracers, levels, rows, width), grad)


def solution(mesh):
    return jax.shard_map(
        on_device,
        mesh=mesh,
        in_specs=(
            P("batch", None, "lat", None),
            P("batch", None, "lat", None),
            P("batch", None, "lat", None),
            P("batch", None, None, "lat", None),
            P(None, "lat"),
            P("batch"),
            P("batch"),
            P("batch"),
            P("batch"),
            P("batch"),
        ),
        out_specs=(P("batch", None, "lat", None), P("lat", None)),
        check_vma=False,
    )
```

```python
import functools
import math

import jax
import jax.numpy as jnp
from jax import lax
from jax.experimental import pallas as pl
from jax.experimental.pallas import tpu as pltpu
from jax.sharding import PartitionSpec as P

HOURS = 2
F32 = jnp.float32
BF16 = jnp.bfloat16
VMEM_LIMIT = 56 * 1024 * 1024


def divisor(value, most):
    return max(d for d in range(1, most + 1) if value % d == 0)


def remote(src, dst, send, recv, where):
    return pltpu.make_async_remote_copy(
        src_ref=src,
        dst_ref=dst,
        send_sem=send,
        recv_sem=recv,
        device_id=where,
        device_id_type=pl.DeviceIdType.MESH,
    )


def faces(courant):
    pos = jnp.maximum(courant, 0.0)
    neg = jnp.minimum(courant, 0.0)
    return pos, neg, pos * (1.0 - pos) * 0.25, neg * (1.0 + neg) * 0.25


def stencil(here, before, before2, after):
    pos, neg, _, neg_slope = faces(here)
    alpha = pos + neg_slope
    _, neg_before, pos_slope_before, _ = faces(before)
    beta = neg_before + pos_slope_before
    q = faces(before2)[3]
    p = faces(after)[2]
    return q, -beta - q, 1.0 - alpha + beta, alpha + p, -p


def kernel(
    n,
    n_lat,
    tracers,
    levels,
    rows,
    block,
    chunk,
    scale,
    adj,
    east,
    north,
    conv,
    owner_table,
    obs_lat,
    obs_lon,
    obs_level,
    obs_hour,
    misfit,
    out,
    grad_out,
    table,
    ring_c,
    north_sel,
    coef_e,
    coef_n,
    send_h,
    halo,
    east_f,
    rounded,
    exch,
    stage_s,
    stage_r,
    mix_b,
    mix_f,
    grad_all,
    s_met,
    r_met,
    s_ring,
    r_ring,
    s_near,
    r_near,
    s_far,
    r_far,
    s_exch,
    r_exch,
    s_stage,
    r_stage,
    s_fwd,
    r_fwd,
    s_grad,
    r_grad,
):
    owner = [owner_table[hour, 0] for hour in range(HOURS)]
    me = lax.axis_index("batch")
    lat = lax.axis_index("lat")
    core = lax.rem(me, 2)
    mate = me + 1 - 2 * core
    bits = []
    bit = 2
    while bit < n:
        bits.append(bit)
        bit *= 2
    n_stage = len(bits)
    half = levels // 2
    n_chunk = half // chunk
    height = levels * rows
    width = adj.shape[-1]
    tiles = height // 8
    n_block = tracers // block
    first = core * half
    other = (1 - core) * half
    up = {"lat": lat + 1}
    down = {"lat": lat - 1}
    has_up = lat < n_lat - 1
    has_down = lat > 0
    odd = lax.rem(lat, 2)
    pair = {"lat": lat + 1 - 2 * odd}
    onward = {"lat": lat + 2 - 4 * odd}
    gives = jnp.where(odd == 0, lat + 2 < n_lat, lat >= 2)
    takes = jnp.where(odd == 0, lat >= 2, lat + 2 < n_lat)

    barrier = pltpu.get_barrier_semaphore()
    for k in range(1, n):
        pl.semaphore_signal(
            barrier, inc=1, device_id={"batch": lax.rem(me + k, n)}, device_id_type=pl.DeviceIdType.MESH
        )

    @pl.when(has_up)
    def _():
        pl.semaphore_signal(barrier, inc=1, device_id=up, device_id_type=pl.DeviceIdType.MESH)

    @pl.when(has_down)
    def _():
        pl.semaphore_signal(barrier, inc=1, device_id=down, device_id_type=pl.DeviceIdType.MESH)

    @pl.when(lat + 2 < n_lat)
    def _():
        pl.semaphore_signal(
            barrier, inc=1, device_id={"lat": lat + 2}, device_id_type=pl.DeviceIdType.MESH
        )

    @pl.when(lat >= 2)
    def _():
        pl.semaphore_signal(
            barrier, inc=1, device_id={"lat": lat - 2}, device_id_type=pl.DeviceIdType.MESH
        )

    greeted = n - 1
    for there in (has_up, has_down, lat + 2 < n_lat, lat >= 2):
        greeted = greeted + jnp.where(there, 1, 0)
    pl.semaphore_wait(barrier, greeted)

    def met_copy(k, i):
        return remote(
            (east, north)[i].at[0],
            table.at[me, i],
            s_met.at[k, i],
            r_met.at[k, i],
            {"batch": lax.rem(me + k, n)},
        )

    for k in range(1, n):
        for i in range(2):
            met_copy(k, i).start()

    def exch_copy(j):
        return remote(
            conv.at[pl.ds(other + j * chunk, chunk)],
            exch.at[pl.ds(j * chunk, chunk)],
            s_exch.at[j],
            r_exch.at[j],
            {"batch": mate},
        )

    for j in range(n_chunk):
        exch_copy(j).start()

    table[me, 0] = east[0]
    table[me, 1] = north[0]

    def zero_halo(side):
        ring_c[side] = jnp.zeros(ring_c.shape[1:], BF16)

        def body(t, carry):
            for hour in range(HOURS):
                halo[hour, side, t] = jnp.zeros(halo.shape[3:], BF16)
            return carry

        lax.fori_loop(0, tracers, body, 0)

    @pl.when(jnp.logical_not(has_down))
    def _():
        zero_halo(0)

    @pl.when(jnp.logical_not(has_up))
    def _():
        zero_halo(1)

    for k in range(1, n):
        for i in range(2):
            met_copy(k, i).wait_recv()

    line = lax.broadcasted_iota(jnp.int32, (height, width), 0)
    lane = lax.broadcasted_iota(jnp.int32, (height, width), 1)
    row_of = lax.rem(line, rows) + lat * rows
    even8 = lax.rem(lax.broadcasted_iota(jnp.int32, (tiles, 8, width), 1), 2) == 0

    def swap(value):
        tall = value.reshape(tiles, 8, width)
        mixed = jnp.where(even8, pltpu.roll(tall, 7, 1), pltpu.roll(tall, 1, 1))
        return mixed.reshape(height, width)

    even = lax.rem(line, 2) == 0

    for hour in range(HOURS):
        cn = table[owner[hour], 1].astype(F32)
        cn = jnp.where(row_of == n_lat * rows - 1, 0.0, cn)
        north_sel[hour] = cn.astype(BF16)

    def ring_copies(side):
        return remote(
            north_sel, ring_c.at[side], s_ring.at[side], r_ring.at[side], up if side == 0 else down
        )

    @pl.when(has_up)
    def _():
        ring_copies(0).start()

    @pl.when(has_down)
    def _():
        ring_copies(1).start()

    for hour in range(HOURS):
        ce = table[owner[hour], 0].astype(F32)
        before = jnp.where(lane >= 1, pltpu.roll(ce, 1, 1), 0.0)
        before2 = jnp.where(lane >= 2, pltpu.roll(ce, 2, 1), 0.0)
        after = jnp.where(lane < width - 1, pltpu.roll(ce, width - 1, 1), 0.0)
        weights = stencil(ce, before, before2, after)
        inside = (lane >= 2, lane >= 1, None, lane < width - 1, lane < width - 2)
        for i, (weight, keep) in enumerate(zip(weights, inside)):
            coef_e[hour, i] = weight if keep is None else jnp.where(keep, weight, 0.0)

    def near_copy(hour, tb):
        at = pl.ds(tb * block, block)
        return remote(
            send_h.at[hour, at],
            halo.at[hour, odd, at],
            s_near.at[hour, tb],
            r_near.at[hour, tb],
            pair,
        )

    def far_copy(hour, tb):
        at = pl.ds(tb * block, block)
        return remote(
            halo.at[hour, 1 - odd, at],
            halo.at[hour, odd, at],
            s_far.at[hour, tb],
            r_far.at[hour, tb],
            onward,
        )

    def relay(hour, tb):
        near_copy(hour, tb).wait_recv()

        @pl.when(gives)
        def _():
            far_copy(hour, tb).start()

    def east_sweep(hour, tb, source):
        def body(i, carry):
            t = tb * block + i
            row_at = obs_lat[t] - lat * rows
            local = (row_at >= 0) & (row_at < rows) & (obs_hour[t] == hour)
            add = jnp.where(local, misfit[t], 0.0)
            hit = (line == obs_level[t] * rows + row_at) & (lane == obs_lon[t])
            field = source[t] + jnp.where(hit, add, 0.0)
            total = coef_e[hour, 2] * field
            total += coef_e[hour, 0] * pltpu.roll(field, 2, 1)
            total += coef_e[hour, 1] * pltpu.roll(field, 1, 1)
            total += coef_e[hour, 3] * pltpu.roll(field, width - 1, 1)
            total += coef_e[hour, 4] * pltpu.roll(field, width - 2, 1)
            east_f[t] = total
            send_h[hour, t] = total.astype(BF16)
            return carry

        lax.fori_loop(0, block, body, 0)

        near_copy(hour, tb).start()

    def north_sweep(hour, tb):
        @pl.when(takes)
        def _():
            far_copy(hour, tb).wait_recv()

        def body(i, carry):
            t = tb * block + i
            field = east_f[t]
            below = halo[hour, 0, t].astype(F32)
            above = halo[hour, 1, t].astype(F32)
            total = coef_n[hour, 0] * below + coef_n[hour, 1] * field
            total += coef_n[hour, 2] * above
            total += coef_n[hour, 3] * swap(field)
            total += coef_n[hour, 4] * swap(jnp.where(even, above, below))
            rounded[t] = total.astype(BF16).astype(F32)
            return carry

        lax.fori_loop(0, block, body, 0)

    even1 = lax.rem(lax.broadcasted_iota(jnp.int32, (1, 8, width), 1), 2) == 0
    part = divisor(tiles, 5)

    def mix(hour, tb, begin, count):
        t_at = pl.ds(tb * block, block)

        def strip(s, carry):
            at = pl.ds(pl.multiple_of(s * part * 8, 8), part * 8)

            def step(j, acc):
                for start in (first, other):
                    for q in range(chunk):
                        m = start + j * chunk + q
                        low = rounded[t_at, pl.ds(2 * m, 1), :]
                        high = rounded[t_at, pl.ds(2 * m + 1, 1), :]
                        both = jnp.where(even1, low, high)
                        matrix = mix_f[hour, m, at, :].reshape(1, part, 8, width)
                        acc = acc + matrix * both[:, None]
                return acc

            shape = (block, part, 8, width)
            if begin == 0:
                acc = jnp.zeros(shape, F32)
            else:
                acc = out[t_at, at, :].reshape(shape)
            if count == 1:
                acc = step(begin, acc)
            else:
                acc = lax.fori_loop(begin, begin + count, step, acc)
            out[t_at, at, :] = acc.reshape(block, part * 8, width)
            return carry

        lax.fori_loop(0, tiles // part, strip, 0)

    def stage_copy(s, hour, j):
        at = pl.ds(j * chunk, chunk)
        bit = bits[s]
        return remote(
            stage_s.at[s, hour, at],
            stage_r.at[s, hour, at],
            s_stage.at[s, hour, j],
            r_stage.at[s, hour, j],
            {"batch": me + bit * (1 - 2 * lax.rem(me // bit, 2))},
        )

    def fwd_copy(hour, j, start):
        at = pl.ds(start + j * chunk, chunk)
        return remote(
            mix_b.at[hour, at],
            mix_b.at[hour, at],
            s_fwd.at[hour, j],
            r_fwd.at[hour, j],
            {"batch": mate},
        )

    def pick(flag, a, b):
        return lax.select(flag, a, b)

    def fill_stage(hour, j):
        at = pl.ds(j * chunk, chunk)
        mine = lax.rem(owner[hour], 2) == core
        stage_s[0, hour, at] = pick(mine, conv[pl.ds(first + j * chunk, chunk)], exch[at])

    def receive(hour, j):
        at = pl.ds(j * chunk, chunk)
        for s in range(n_stage):
            bit = bits[s]
            mine = lax.rem(owner[hour] // bit, 2) == lax.rem(me // bit, 2)
            stage_copy(s, hour, j).wait_recv()
            value = pick(mine, stage_s[s, hour, at], stage_r[s, hour, at])
            if s + 1 < n_stage:
                stage_s[s + 1, hour, at] = value
                stage_copy(s + 1, hour, j).start()
            else:
                mix_b[hour, pl.ds(first + j * chunk, chunk)] = value
                fwd_copy(hour, j, first).start()
                mix_f[hour, pl.ds(first + j * chunk, chunk)] = value.astype(F32)
            if s == 0 and hour > 0:
                stage_copy(0, hour - 1, j).start()

    def widen(hour, j):
        at = pl.ds(other + j * chunk, chunk)
        fwd_copy(hour, j, other).wait_recv()
        mix_f[hour, at] = mix_b[hour, at].astype(F32)

    last = HOURS - 1
    def start_stage(j):
        exch_copy(j).wait_recv()
        fill_stage(last, j)
        stage_copy(0, last, j).start()

    for tb in range(max(n_block, n_chunk)):
        if tb < n_chunk:
            start_stage(tb)
        if tb < n_block:
            east_sweep(last, tb, adj)

    def fill_later(j, carry):
        for hour in range(last):
            fill_stage(hour, j)
        return carry

    lax.fori_loop(0, n_chunk, fill_later, 0)

    @pl.when(has_down)
    def _():
        ring_copies(0).wait_recv()

    @pl.when(has_up)
    def _():
        ring_copies(1).wait_recv()

    for hour in range(HOURS):
        here = north_sel[hour].astype(F32)
        below = ring_c[0, hour].astype(F32)
        above = ring_c[1, hour].astype(F32)
        turned = swap(here)
        crossed = swap(jnp.where(even, above, below))
        before = jnp.where(even, crossed, turned)
        after = jnp.where(even, turned, crossed)
        w_m2, w_m1, w_0, w_p1, w_p2 = stencil(here, before, below, after)
        coef_n[hour, 0] = w_m2
        coef_n[hour, 1] = w_0
        coef_n[hour, 2] = w_p2
        coef_n[hour, 3] = jnp.where(even, w_p1, w_m1)
        coef_n[hour, 4] = jnp.where(even, w_m1, w_p1)

    bulk = n_chunk - 2
    surface = jnp.zeros((8, width), F32)
    for hour in reversed(range(HOURS)):
        for j in range(max(bulk, n_block)):
            if j < n_block:
                relay(hour, j)
            if j < bulk:
                receive(hour, j)
        for j in range(bulk):
            widen(hour, j)
        for tb in range(n_block):
            north_sweep(hour, tb)
            mix(hour, tb, 0, bulk)
        for j in range(bulk, n_chunk):
            receive(hour, j)
            widen(hour, j)
            for tb in range(n_block):
                mix(hour, tb, j, 1)
                if j < n_chunk - 1:
                    continue
                for i in range(block):
                    surface = surface + out[tb * block + i, 0:8, :]
                if hour > 0:
                    east_sweep(hour - 1, tb, out)

    grad_all[me] = surface

    def grad_copy(k):
        return remote(
            grad_all.at[me],
            grad_all.at[me],
            s_grad.at[k],
            r_grad.at[k],
            {"batch": lax.rem(me + k, n)},
        )

    for k in range(1, n):
        grad_copy(k).start()

    for k in range(1, n):
        for i in range(2):
            met_copy(k, i).wait_send()

    @pl.when(has_up)
    def _():
        ring_copies(0).wait_send()

    @pl.when(has_down)
    def _():
        ring_copies(1).wait_send()

    for hour in range(HOURS):
        for tb in range(n_block):
            near_copy(hour, tb).wait_send()

    @pl.when(gives)
    def _():
        for hour in range(HOURS):
            for tb in range(n_block):
                far_copy(hour, tb).wait_send()

    def drain(j, carry):
        exch_copy(j).wait_send()
        for hour in range(HOURS):
            for s in range(n_stage):
                stage_copy(s, hour, j).wait_send()
            fwd_copy(hour, j, first).wait_send()
        return carry

    lax.fori_loop(0, n_chunk, drain, 0)
    for k in range(1, n):
        grad_copy(k).wait_recv()
    for k in range(1, n):
        grad_copy(k).wait_send()
    total = grad_all[0]
    for k in range(1, n):
        total = total + grad_all[k]
    grad_out[...] = total[0:rows] * scale


def on_device(
    adjoint_in,
    east_courant,
    north_courant,
    convection,
    hour_owner,
    obs_lat,
    obs_lon,
    obs_level,
    obs_hour,
    misfit,
):
    tracers, levels, rows, width = adjoint_in.shape
    n = lax.axis_size("batch")
    n_lat = lax.axis_size("lat")
    height = levels * rows
    block = divisor(tracers, 5)
    half = levels // 2
    chunk = divisor(half, 5)
    n_chunk = half // chunk
    n_block = tracers // block
    n_stage = n.bit_length() - 2
    scale = 1.0 / math.sqrt(tracers * n)
    vmem = pl.BlockSpec(memory_space=pltpu.VMEM)
    smem = pl.BlockSpec(memory_space=pltpu.SMEM)
    dma = pltpu.SemaphoreType.DMA
    body = functools.partial(
        kernel, n, n_lat, tracers, levels, rows, block, chunk, scale
    )
    out, grad = pl.pallas_call(
        body,
        out_shape=(
            jax.ShapeDtypeStruct((tracers, height, width), F32),
            jax.ShapeDtypeStruct((rows, width), F32),
        ),
        in_specs=[vmem] * 4 + [smem] * 6,
        out_specs=(vmem, vmem),
        scratch_shapes=[
            pltpu.VMEM((n, 2, height, width), BF16),
            pltpu.VMEM((2, HOURS, height, width), BF16),
            pltpu.VMEM((HOURS, height, width), BF16),
            pltpu.VMEM((HOURS, 5, height, width), F32),
            pltpu.VMEM((HOURS, 5, height, width), F32),
            pltpu.VMEM((HOURS, tracers, height, width), BF16),
            pltpu.VMEM((HOURS, 2, tracers, height, width), BF16),
            pltpu.VMEM((tracers, height, width), F32),
            pltpu.VMEM((tracers, height, width), F32),
            pltpu.VMEM((half, height, width), BF16),
            pltpu.VMEM((n_stage, HOURS, half, height, width), BF16),
            pltpu.VMEM((n_stage, HOURS, half, height, width), BF16),
            pltpu.VMEM((HOURS, levels, height, width), BF16),
            pltpu.VMEM((HOURS, levels, height, width), F32),
            pltpu.VMEM((n, 8, width), F32),
            dma((n, 2)),
            dma((n, 2)),
            dma((2,)),
            dma((2,)),
            dma((HOURS, n_block)),
            dma((HOURS, n_block)),
            dma((HOURS, n_block)),
            dma((HOURS, n_block)),
            dma((n_chunk,)),
            dma((n_chunk,)),
            dma((n_stage, HOURS, n_chunk)),
            dma((n_stage, HOURS, n_chunk)),
            dma((HOURS, n_chunk)),
            dma((HOURS, n_chunk)),
            dma((n,)),
            dma((n,)),
        ],
        compiler_params=pltpu.CompilerParams(
            collective_id=0, has_side_effects=True, vmem_limit_bytes=VMEM_LIMIT
        ),
    )(
        adjoint_in.reshape(tracers, height, width),
        east_courant.reshape(1, height, width),
        north_courant.reshape(1, height, width),
        convection.reshape(levels, height, width),
        hour_owner,
        obs_lat,
        obs_lon,
        obs_level,
        obs_hour,
        misfit,
    )
    return (out.reshape(tracers, levels, rows, width), grad)


def solution(mesh):
    return jax.shard_map(
        on_device,
        mesh=mesh,
        in_specs=(
            P("batch", None, "lat", None),
            P("batch", None, "lat", None),
            P("batch", None, "lat", None),
            P("batch", None, None, "lat", None),
            P(None, "lat"),
            P("batch"),
            P("batch"),
            P("batch"),
            P("batch"),
            P("batch"),
        ),
        out_specs=(P("batch", None, "lat", None), P("lat", None)),
        check_vma=False,
    )
```

```python
import functools
import math

import jax
import jax.numpy as jnp
from jax import lax
from jax.experimental import pallas as pl
from jax.experimental.pallas import tpu as pltpu
from jax.sharding import PartitionSpec as P

HOURS = 2
F32 = jnp.float32
BF16 = jnp.bfloat16
VMEM_LIMIT = 56 * 1024 * 1024


def divisor(value, most):
    return max(d for d in range(1, most + 1) if value % d == 0)


def remote(src, dst, send, recv, where):
    return pltpu.make_async_remote_copy(
        src_ref=src,
        dst_ref=dst,
        send_sem=send,
        recv_sem=recv,
        device_id=where,
        device_id_type=pl.DeviceIdType.MESH,
    )


def faces(courant):
    pos = jnp.maximum(courant, 0.0)
    neg = jnp.minimum(courant, 0.0)
    return pos, neg, pos * (1.0 - pos) * 0.25, neg * (1.0 + neg) * 0.25


def stencil(here, before, before2, after):
    pos, neg, _, neg_slope = faces(here)
    alpha = pos + neg_slope
    _, neg_before, pos_slope_before, _ = faces(before)
    beta = neg_before + pos_slope_before
    q = faces(before2)[3]
    p = faces(after)[2]
    return q, -beta - q, 1.0 - alpha + beta, alpha + p, -p


def kernel(
    n,
    n_lat,
    tracers,
    levels,
    rows,
    block,
    chunk,
    scale,
    adj,
    east,
    north,
    conv,
    owner_table,
    obs_lat,
    obs_lon,
    obs_level,
    obs_hour,
    misfit,
    result,
    grad_out,
    out,
    own,
    table,
    ring_c,
    north_sel,
    coef_e,
    coef_n,
    send_h,
    halo,
    east_f,
    rounded,
    exch,
    stage_s,
    stage_r,
    mix_b,
    mix_f,
    grad_all,
    s_met,
    r_met,
    s_ring,
    r_ring,
    s_near,
    r_near,
    s_far,
    r_far,
    s_exch,
    r_exch,
    s_stage,
    r_stage,
    s_fwd,
    r_fwd,
    s_grad,
    r_grad,
    s_own,
    s_adj,
    s_out,
):
    owner = [owner_table[hour, 0] for hour in range(HOURS)]
    me = lax.axis_index("batch")
    lat = lax.axis_index("lat")
    core = lax.rem(me, 2)
    mate = me + 1 - 2 * core
    bits = []
    bit = 2
    while bit < n:
        bits.append(bit)
        bit *= 2
    n_stage = len(bits)
    half = levels // 2
    n_chunk = half // chunk
    height = levels * rows
    width = adj.shape[-1]
    tiles = height // 8
    n_block = tracers // block
    first = core * half
    other = (1 - core) * half
    up = {"lat": lat + 1}
    down = {"lat": lat - 1}
    has_up = lat < n_lat - 1
    has_down = lat > 0
    odd = lax.rem(lat, 2)
    pair = {"lat": lat + 1 - 2 * odd}
    onward = {"lat": lat + 2 - 4 * odd}
    gives = jnp.where(odd == 0, lat + 2 < n_lat, lat >= 2)
    takes = jnp.where(odd == 0, lat >= 2, lat + 2 < n_lat)

    def own_copy(j):
        at = pl.ds(j * chunk, chunk)
        return pltpu.make_async_copy(conv.at[pl.ds(first + j * chunk, chunk)], own.at[at], s_own.at[j])

    def adj_copy(tb):
        at = pl.ds(tb * block, block)
        return pltpu.make_async_copy(adj.at[at], out.at[at], s_adj.at[tb])

    def out_copy(tb):
        at = pl.ds(tb * block, block)
        return pltpu.make_async_copy(out.at[at], result.at[at], s_out.at[tb])

    for j in range(n_chunk):
        own_copy(j).start()
    for tb in range(n_block):
        adj_copy(tb).start()

    barrier = pltpu.get_barrier_semaphore()
    for k in range(1, n):
        pl.semaphore_signal(
            barrier, inc=1, device_id={"batch": lax.rem(me + k, n)}, device_id_type=pl.DeviceIdType.MESH
        )

    @pl.when(has_up)
    def _():
        pl.semaphore_signal(barrier, inc=1, device_id=up, device_id_type=pl.DeviceIdType.MESH)

    @pl.when(has_down)
    def _():
        pl.semaphore_signal(barrier, inc=1, device_id=down, device_id_type=pl.DeviceIdType.MESH)

    @pl.when(lat + 2 < n_lat)
    def _():
        pl.semaphore_signal(
            barrier, inc=1, device_id={"lat": lat + 2}, device_id_type=pl.DeviceIdType.MESH
        )

    @pl.when(lat >= 2)
    def _():
        pl.semaphore_signal(
            barrier, inc=1, device_id={"lat": lat - 2}, device_id_type=pl.DeviceIdType.MESH
        )

    greeted = n - 1
    for there in (has_up, has_down, lat + 2 < n_lat, lat >= 2):
        greeted = greeted + jnp.where(there, 1, 0)
    pl.semaphore_wait(barrier, greeted)

    def met_copy(k, i):
        return remote(
            (east, north)[i].at[0],
            table.at[me, i],
            s_met.at[k, i],
            r_met.at[k, i],
            {"batch": lax.rem(me + k, n)},
        )

    for k in range(1, n):
        for i in range(2):
            met_copy(k, i).start()

    def exch_copy(j):
        return remote(
            conv.at[pl.ds(other + j * chunk, chunk)],
            exch.at[pl.ds(j * chunk, chunk)],
            s_exch.at[j],
            r_exch.at[j],
            {"batch": mate},
        )

    for j in range(n_chunk):
        exch_copy(j).start()

    table[me, 0] = east[0]
    table[me, 1] = north[0]

    def zero_halo(side):
        ring_c[side] = jnp.zeros(ring_c.shape[1:], BF16)

        def body(t, carry):
            for hour in range(HOURS):
                halo[hour, side, t] = jnp.zeros(halo.shape[3:], BF16)
            return carry

        lax.fori_loop(0, tracers, body, 0)

    @pl.when(jnp.logical_not(has_down))
    def _():
        zero_halo(0)

    @pl.when(jnp.logical_not(has_up))
    def _():
        zero_halo(1)

    def stage_copy(s, hour, j):
        at = pl.ds(j * chunk, chunk)
        bit = bits[s]
        return remote(
            stage_s.at[s, hour, at],
            stage_r.at[s, hour, at],
            s_stage.at[s, hour, j],
            r_stage.at[s, hour, j],
            {"batch": me + bit * (1 - 2 * lax.rem(me // bit, 2))},
        )

    def fwd_copy(hour, j, start):
        at = pl.ds(start + j * chunk, chunk)
        return remote(
            mix_b.at[hour, at],
            mix_b.at[hour, at],
            s_fwd.at[hour, j],
            r_fwd.at[hour, j],
            {"batch": mate},
        )

    def pick(flag, a, b):
        return lax.select(flag, a, b)

    def fill_stage(hour, j):
        at = pl.ds(j * chunk, chunk)
        mine = lax.rem(owner[hour], 2) == core
        stage_s[0, hour, at] = pick(mine, own[at], exch[at])

    last = HOURS - 1
    lead = 2

    def start_stage(j):
        own_copy(j).wait()
        exch_copy(j).wait_recv()
        fill_stage(last, j)
        stage_copy(0, last, j).start()

    for j in range(lead):
        start_stage(j)

    for k in range(1, n):
        for i in range(2):
            met_copy(k, i).wait_recv()

    line = lax.broadcasted_iota(jnp.int32, (height, width), 0)
    lane = lax.broadcasted_iota(jnp.int32, (height, width), 1)
    row_of = lax.rem(line, rows) + lat * rows
    even8 = lax.rem(lax.broadcasted_iota(jnp.int32, (tiles, 8, width), 1), 2) == 0

    def swap(value):
        tall = value.reshape(tiles, 8, width)
        mixed = jnp.where(even8, pltpu.roll(tall, 7, 1), pltpu.roll(tall, 1, 1))
        return mixed.reshape(height, width)

    even = lax.rem(line, 2) == 0

    for hour in range(HOURS):
        cn = table[owner[hour], 1].astype(F32)
        cn = jnp.where(row_of == n_lat * rows - 1, 0.0, cn)
        north_sel[hour] = cn.astype(BF16)

    def ring_copies(side):
        return remote(
            north_sel, ring_c.at[side], s_ring.at[side], r_ring.at[side], up if side == 0 else down
        )

    @pl.when(has_up)
    def _():
        ring_copies(0).start()

    @pl.when(has_down)
    def _():
        ring_copies(1).start()

    def set_east(hour):
        ce = table[owner[hour], 0].astype(F32)
        before = jnp.where(lane >= 1, pltpu.roll(ce, 1, 1), 0.0)
        before2 = jnp.where(lane >= 2, pltpu.roll(ce, 2, 1), 0.0)
        after = jnp.where(lane < width - 1, pltpu.roll(ce, width - 1, 1), 0.0)
        weights = stencil(ce, before, before2, after)
        inside = (lane >= 2, lane >= 1, None, lane < width - 1, lane < width - 2)
        for i, (weight, keep) in enumerate(zip(weights, inside)):
            coef_e[hour, i] = weight if keep is None else jnp.where(keep, weight, 0.0)

    set_east(last)

    def near_copy(hour, tb):
        at = pl.ds(tb * block, block)
        return remote(
            send_h.at[hour, at],
            halo.at[hour, odd, at],
            s_near.at[hour, tb],
            r_near.at[hour, tb],
            pair,
        )

    def far_copy(hour, tb):
        at = pl.ds(tb * block, block)
        return remote(
            halo.at[hour, 1 - odd, at],
            halo.at[hour, odd, at],
            s_far.at[hour, tb],
            r_far.at[hour, tb],
            onward,
        )

    def relay(hour, tb):
        near_copy(hour, tb).wait_recv()

        @pl.when(gives)
        def _():
            far_copy(hour, tb).start()

    def east_sweep(hour, tb, source):
        def body(i, carry):
            t = tb * block + i
            row_at = obs_lat[t] - lat * rows
            local = (row_at >= 0) & (row_at < rows) & (obs_hour[t] == hour)
            add = jnp.where(local, misfit[t], 0.0)
            hit = (line == obs_level[t] * rows + row_at) & (lane == obs_lon[t])
            field = source[t] + jnp.where(hit, add, 0.0)
            total = coef_e[hour, 2] * field
            total += coef_e[hour, 0] * pltpu.roll(field, 2, 1)
            total += coef_e[hour, 1] * pltpu.roll(field, 1, 1)
            total += coef_e[hour, 3] * pltpu.roll(field, width - 1, 1)
            total += coef_e[hour, 4] * pltpu.roll(field, width - 2, 1)
            east_f[t] = total
            send_h[hour, t] = total.astype(BF16)
            return carry

        lax.fori_loop(0, block, body, 0)

        near_copy(hour, tb).start()

    def north_sweep(hour, tb):
        @pl.when(takes)
        def _():
            far_copy(hour, tb).wait_recv()

        def body(i, carry):
            t = tb * block + i
            field = east_f[t]
            below = halo[hour, 0, t].astype(F32)
            above = halo[hour, 1, t].astype(F32)
            total = coef_n[hour, 0] * below + coef_n[hour, 1] * field
            total += coef_n[hour, 2] * above
            total += coef_n[hour, 3] * swap(field)
            total += coef_n[hour, 4] * swap(jnp.where(even, above, below))
            rounded[t] = total.astype(BF16).astype(F32)
            return carry

        lax.fori_loop(0, block, body, 0)

    even1 = lax.rem(lax.broadcasted_iota(jnp.int32, (1, 8, width), 1), 2) == 0
    part = divisor(tiles, 5)

    def mix(hour, tb, begin, count):
        t_at = pl.ds(tb * block, block)

        def strip(s, carry):
            at = pl.ds(pl.multiple_of(s * part * 8, 8), part * 8)

            def step(j, acc):
                for start in (first, other):
                    for q in range(chunk):
                        m = start + j * chunk + q
                        low = rounded[t_at, pl.ds(2 * m, 1), :]
                        high = rounded[t_at, pl.ds(2 * m + 1, 1), :]
                        both = jnp.where(even1, low, high)
                        matrix = mix_f[hour, m, at, :].reshape(1, part, 8, width)
                        acc = acc + matrix * both[:, None]
                return acc

            shape = (block, part, 8, width)
            if begin == 0:
                acc = jnp.zeros(shape, F32)
            else:
                acc = out[t_at, at, :].reshape(shape)
            if count == 1:
                acc = step(begin, acc)
            else:
                acc = lax.fori_loop(begin, begin + count, step, acc)
            out[t_at, at, :] = acc.reshape(block, part * 8, width)
            return carry

        lax.fori_loop(0, tiles // part, strip, 0)

    def receive(hour, j):
        at = pl.ds(j * chunk, chunk)
        for s in range(n_stage):
            bit = bits[s]
            mine = lax.rem(owner[hour] // bit, 2) == lax.rem(me // bit, 2)
            stage_copy(s, hour, j).wait_recv()
            value = pick(mine, stage_s[s, hour, at], stage_r[s, hour, at])
            if s + 1 < n_stage:
                stage_s[s + 1, hour, at] = value
                stage_copy(s + 1, hour, j).start()
            else:
                mix_b[hour, pl.ds(first + j * chunk, chunk)] = value
                fwd_copy(hour, j, first).start()
                mix_f[hour, pl.ds(first + j * chunk, chunk)] = value.astype(F32)
            if s == 0 and hour > 0:
                stage_copy(0, hour - 1, j).start()

    def widen(hour, j):
        at = pl.ds(other + j * chunk, chunk)
        fwd_copy(hour, j, other).wait_recv()
        mix_f[hour, at] = mix_b[hour, at].astype(F32)

    for tb in range(max(n_block, n_chunk)):
        if tb + lead < n_chunk:
            start_stage(tb + lead)
        if tb < n_block:
            adj_copy(tb).wait()
            east_sweep(last, tb, out)

    def fill_later(j, carry):
        for hour in range(last):
            fill_stage(hour, j)
        return carry

    lax.fori_loop(0, n_chunk, fill_later, 0)

    @pl.when(has_down)
    def _():
        ring_copies(0).wait_recv()

    @pl.when(has_up)
    def _():
        ring_copies(1).wait_recv()

    def set_north(hour):
        here = north_sel[hour].astype(F32)
        below = ring_c[0, hour].astype(F32)
        above = ring_c[1, hour].astype(F32)
        turned = swap(here)
        crossed = swap(jnp.where(even, above, below))
        before = jnp.where(even, crossed, turned)
        after = jnp.where(even, turned, crossed)
        w_m2, w_m1, w_0, w_p1, w_p2 = stencil(here, before, below, after)
        coef_n[hour, 0] = w_m2
        coef_n[hour, 1] = w_0
        coef_n[hour, 2] = w_p2
        coef_n[hour, 3] = jnp.where(even, w_p1, w_m1)
        coef_n[hour, 4] = jnp.where(even, w_m1, w_p1)

    set_north(last)
    bulk = n_chunk - 2
    surface = jnp.zeros((8, width), F32)
    for hour in reversed(range(HOURS)):
        for j in range(max(bulk, n_block)):
            if j < n_block:
                relay(hour, j)
            if j < bulk:
                receive(hour, j)
        for j in range(bulk):
            widen(hour, j)
        for tb in range(n_block):
            north_sweep(hour, tb)
            mix(hour, tb, 0, bulk)
        if hour > 0:
            set_east(hour - 1)
            set_north(hour - 1)
        for j in range(bulk, n_chunk):
            receive(hour, j)
            widen(hour, j)
            for tb in range(n_block):
                mix(hour, tb, j, 1)
                if j < n_chunk - 1:
                    continue
                for i in range(block):
                    surface = surface + out[tb * block + i, 0:8, :]
                if hour > 0:
                    east_sweep(hour - 1, tb, out)
                else:
                    out_copy(tb).start()

    grad_all[me] = surface

    def grad_copy(k):
        return remote(
            grad_all.at[me],
            grad_all.at[me],
            s_grad.at[k],
            r_grad.at[k],
            {"batch": lax.rem(me + k, n)},
        )

    for k in range(1, n):
        grad_copy(k).start()

    for k in range(1, n):
        for i in range(2):
            met_copy(k, i).wait_send()

    @pl.when(has_up)
    def _():
        ring_copies(0).wait_send()

    @pl.when(has_down)
    def _():
        ring_copies(1).wait_send()

    for hour in range(HOURS):
        for tb in range(n_block):
            near_copy(hour, tb).wait_send()

    @pl.when(gives)
    def _():
        for hour in range(HOURS):
            for tb in range(n_block):
                far_copy(hour, tb).wait_send()

    def drain(j, carry):
        exch_copy(j).wait_send()
        for hour in range(HOURS):
            for s in range(n_stage):
                stage_copy(s, hour, j).wait_send()
            fwd_copy(hour, j, first).wait_send()
        return carry

    lax.fori_loop(0, n_chunk, drain, 0)
    for tb in range(n_block):
        out_copy(tb).wait()
    for k in range(1, n):
        grad_copy(k).wait_recv()
    for k in range(1, n):
        grad_copy(k).wait_send()
    total = grad_all[0]
    for k in range(1, n):
        total = total + grad_all[k]
    grad_out[...] = total[0:rows] * scale


def on_device(
    adjoint_in,
    east_courant,
    north_courant,
    convection,
    hour_owner,
    obs_lat,
    obs_lon,
    obs_level,
    obs_hour,
    misfit,
):
    tracers, levels, rows, width = adjoint_in.shape
    n = lax.axis_size("batch")
    n_lat = lax.axis_size("lat")
    height = levels * rows
    block = divisor(tracers, 5)
    half = levels // 2
    chunk = divisor(half, 5)
    n_chunk = half // chunk
    n_block = tracers // block
    n_stage = n.bit_length() - 2
    scale = 1.0 / math.sqrt(tracers * n)
    vmem = pl.BlockSpec(memory_space=pltpu.VMEM)
    hbm = pl.BlockSpec(memory_space=pl.ANY)
    smem = pl.BlockSpec(memory_space=pltpu.SMEM)
    dma = pltpu.SemaphoreType.DMA
    body = functools.partial(
        kernel, n, n_lat, tracers, levels, rows, block, chunk, scale
    )
    out, grad = pl.pallas_call(
        body,
        out_shape=(
            jax.ShapeDtypeStruct((tracers, height, width), F32),
            jax.ShapeDtypeStruct((rows, width), F32),
        ),
        in_specs=[hbm, vmem, vmem, hbm] + [smem] * 6,
        out_specs=(hbm, vmem),
        scratch_shapes=[
            pltpu.VMEM((tracers, height, width), F32),
            pltpu.VMEM((half, height, width), BF16),
            pltpu.VMEM((n, 2, height, width), BF16),
            pltpu.VMEM((2, HOURS, height, width), BF16),
            pltpu.VMEM((HOURS, height, width), BF16),
            pltpu.VMEM((HOURS, 5, height, width), F32),
            pltpu.VMEM((HOURS, 5, height, width), F32),
            pltpu.VMEM((HOURS, tracers, height, width), BF16),
            pltpu.VMEM((HOURS, 2, tracers, height, width), BF16),
            pltpu.VMEM((tracers, height, width), F32),
            pltpu.VMEM((tracers, height, width), F32),
            pltpu.VMEM((half, height, width), BF16),
            pltpu.VMEM((n_stage, HOURS, half, height, width), BF16),
            pltpu.VMEM((n_stage, HOURS, half, height, width), BF16),
            pltpu.VMEM((HOURS, levels, height, width), BF16),
            pltpu.VMEM((HOURS, levels, height, width), F32),
            pltpu.VMEM((n, 8, width), F32),
            dma((n, 2)),
            dma((n, 2)),
            dma((2,)),
            dma((2,)),
            dma((HOURS, n_block)),
            dma((HOURS, n_block)),
            dma((HOURS, n_block)),
            dma((HOURS, n_block)),
            dma((n_chunk,)),
            dma((n_chunk,)),
            dma((n_stage, HOURS, n_chunk)),
            dma((n_stage, HOURS, n_chunk)),
            dma((HOURS, n_chunk)),
            dma((HOURS, n_chunk)),
            dma((n,)),
            dma((n,)),
            dma((n_chunk,)),
            dma((n_block,)),
            dma((n_block,)),
        ],
        compiler_params=pltpu.CompilerParams(
            collective_id=0, has_side_effects=True, vmem_limit_bytes=VMEM_LIMIT
        ),
    )(
        adjoint_in.reshape(tracers, height, width),
        east_courant.reshape(1, height, width),
        north_courant.reshape(1, height, width),
        convection.reshape(levels, height, width),
        hour_owner,
        obs_lat,
        obs_lon,
        obs_level,
        obs_hour,
        misfit,
    )
    return (out.reshape(tracers, levels, rows, width), grad)


def solution(mesh):
    return jax.shard_map(
        on_device,
        mesh=mesh,
        in_specs=(
            P("batch", None, "lat", None),
            P("batch", None, "lat", None),
            P("batch", None, "lat", None),
            P("batch", None, None, "lat", None),
            P(None, "lat"),
            P("batch"),
            P("batch"),
            P("batch"),
            P("batch"),
            P("batch"),
        ),
        out_specs=(P("batch", None, "lat", None), P("lat", None)),
        check_vma=False,
    )
```
